32 devices in a mesh: grp: 2 (over y), space: 4 (over z), chaos: 2 (over x), mode: 2 (over core).
Axes of the slice: x: 2, y: 2, z: 4, core: 2. Of those that a mesh axis runs over, the one named last changes fastest.
Arguments:
- coeffs: bfloat16 [8, 48, 16384], P(None, 'chaos', ('grp', 'space')), parts along dimension 2, may hold values from -6 to 6
- tangent: bfloat16 [8, 128, 3, 128, 128], P('mode', ('grp', 'space')), parts along dimension 1, may hold values from -0.3125 to 0.3125
- block_cols: int32 [128, 3], P(('grp', 'space')), parts along dimension 0, may hold values from 0 to 63, as said below
- galerkin: float32 [8, 48, 48], replicated, may hold values from -2.5 to 3
- galerkin_mask: int32 [8, 48, 48], replicated, may hold values 0 or 1
Outputs:
- applied: bfloat16 [8, 48, 16384], P(None, ('chaos', 'mode'), ('grp', 'space')), parts along dimension 2
The draws below stay inside these ranges and needn't reach their ends.
There are 2 independent parts, one for each index of `grp`. The reference program is written for one: setup_inputs(seed, part) draws one part's arguments, and reference() takes and returns one part's arrays. A program takes and returns all parts, laid end to end along the dimension named above; an argument that names none is the same for every part. Nothing has to cross between parts.
Inputs may be any that keep to these rules, and one draw needn't show every extreme that they name: `block_cols`: each row holds its own block index first, then two other block indices at cyclic distance 1 or 2 from it (modulo 64); the three are distinct.
All inputs are finite; a program needn't handle non-finite values.
Results may differ from the reference program's by a relative error of at most 0.001.
Values may be sent and summed in bfloat16 or wider, within the bound.
A program may use at most 192 MiB of HBM per device.

```python
import jax
import jax.numpy as jnp
import numpy as np
from jax import lax

P_SIZE = 48
MODES = 8
BLK = 128
NNZ = 3
FIELDS = 8
NBLK = 64
NDOF = 8192


def draw_block_cols(key, part):
    key = jax.random.fold_in(key, 11)
    scores = jax.random.randint(key, (NBLK, 4), 0, 4096) * 4 + jnp.arange(4, dtype=jnp.int32)[None, :]
    picked = jnp.argsort(scores, axis=1)[:, :2]
    steps_table = jnp.array(np.array([-2, -1, 1, 2], dtype=np.int32))
    offsets = steps_table[picked]
    own_rows = jnp.arange(NBLK, dtype=jnp.int32)[:, None]
    others = (own_rows + offsets + NBLK) % NBLK
    return jnp.concatenate([own_rows, others], axis=1).astype(jnp.int32)


def draw_galerkin(key, part):
    key = jax.random.fold_in(key, 5)
    first_key, second_key = jax.random.split(key)
    spread = jax.random.truncated_normal(first_key, -3.0, 3.0, (MODES, P_SIZE, P_SIZE), jnp.float32)
    diagonal = jax.random.uniform(second_key, (MODES, P_SIZE), jnp.float32, 0.8, 1.6)
    eye_table = jnp.eye(P_SIZE, dtype=jnp.float32)
    values = spread * (0.6 / P_SIZE ** 0.5) * (1.0 - eye_table)[None] + eye_table[None] * diagonal[:, :, None]
    return values.astype(jnp.float32)


def with_ends(values, own_key, smallest, high):
    spot = [jax.random.randint(jax.random.fold_in(own_key, axis), (), 0, length) for axis, length in enumerate(values.shape)]
    longest = values.shape.index(max(values.shape))
    neighbour = spot[:longest] + [(spot[longest] + 1) % values.shape[longest]] + spot[longest + 1:]
    return values.at[tuple(spot)].set(smallest).at[tuple(neighbour)].set(high)


def levels(own_key, dims, cuts, low, largest):
    level = 1.0
    for position, parts in cuts:
        draws = jax.random.uniform(jax.random.fold_in(jax.random.fold_in(own_key, 6), position), (parts,), jnp.float32, low / len(cuts), largest / len(cuts))
        level = level * jnp.repeat(jnp.exp(draws), dims[position] // parts).reshape((-1,) + (1,) * (len(dims) - 1 - position))
    return level


def normal_values(rng, extent, width, most, shards=(), held_as=jnp.bfloat16):
    values = width * jax.random.normal(rng, extent, jnp.float32)
    if shards:
        values = values * levels(rng, extent, shards, -0.22, 0.18)
    return jnp.clip(values, -most, most).astype(held_as)


def setup_inputs(seed: int = 0, part: int = 0) -> dict:
    streams_of = jax.random.split(jax.random.key(seed), 6)
    part_splits = jax.random.split(jax.random.fold_in(streams_of[5], part), 6)
    return {
        "coeffs": normal_values(part_splits[0], (FIELDS, P_SIZE, NDOF), 1.0, 6.0, ((1, 2), (2, 4))),
        "tangent": normal_values(part_splits[1], (MODES, NBLK, NNZ, BLK, BLK), (NNZ * BLK) ** -0.5, 0.3125, ((0, 2), (1, 4))),
        "block_cols": draw_block_cols(jax.random.fold_in(jax.random.fold_in(streams_of[5], part), 71), part),
        "galerkin": draw_galerkin(jax.random.fold_in(streams_of[5], 71), part),
        "galerkin_mask": with_ends((jax.random.randint(streams_of[4], (MODES, P_SIZE, P_SIZE), 0, 2) < 1).astype(jnp.int32), jax.random.fold_in(streams_of[4], 1), 0, 1),
    }


def reference(coeffs, tangent, block_cols, galerkin, galerkin_mask):
    first = lax.broadcasted_iota(jnp.int32, (MODES, P_SIZE, P_SIZE), 1)
    second = lax.broadcasted_iota(jnp.int32, (MODES, P_SIZE, P_SIZE), 2)
    keep = (first == second) | (galerkin_mask == 1)
    mixing = jnp.where(keep, galerkin, jnp.zeros_like(galerkin))
    blocks = coeffs.astype(jnp.float32).reshape(FIELDS, P_SIZE, NBLK, BLK)
    result = jnp.zeros((FIELDS, P_SIZE, NBLK, BLK), jnp.float32)
    for index in range(MODES):
        contrib = jnp.einsum("fqrb,rnbc->fqrnc", blocks, tangent[index].astype(jnp.float32), precision=lax.Precision.HIGHEST)
        image = jnp.zeros((FIELDS, P_SIZE, NBLK, BLK), jnp.float32).at[:, :, block_cols].add(contrib)
        result = result + jnp.einsum("qp,fqjc->fpjc", mixing[index], image, precision=lax.Precision.HIGHEST)
    return result.reshape(FIELDS, P_SIZE, NBLK * BLK).astype(jnp.bfloat16)
```

```python
import functools

import jax
import jax.numpy as jnp
import numpy as np
from jax import lax
from jax.experimental import pallas as pl
from jax.experimental.pallas import tpu as pltpu
from jax.sharding import PartitionSpec as P

REACH = 2
MESH = pl.DeviceIdType.MESH
F32 = jnp.float32
BF16 = jnp.bfloat16


def group_of(fields, rows_in, own_p):
    for group in range(1, fields + 1):
        if fields % group == 0 and group * rows_in % 16 == 0 and group * own_p % 8 == 0:
            return group
    return fields


def kernel(dims, cols_ref, x_hbm, t_hbm, g_hbm, gm_hbm, spread_ref, same_ref, half_ref, place_ref, perm_ref,
           out_ref, x_all, t_all, g_all, gm_all, mix, z, contrib, part, recv, rim, halo,
           local_sem, xs, xr, fs, fr, ys, yr, hs, hr):
    n, space_size, fields, rows_in, own_p, group, modes, block_rows, slots, blk = dims
    chaos = lax.axis_index("chaos")
    mode = lax.axis_index("mode")
    space = lax.axis_index("space")
    other = 1 - mode
    above = lax.rem(space + 1, space_size)
    below = lax.rem(space + space_size - 1, space_size)
    span = block_rows + 2 * REACH
    chunks = block_rows // 2
    pairs = span // 2
    rows = fields * own_p
    p_size = n * rows_in
    shell = block_rows * space_size
    zero_at = block_rows * slots

    locals_ = [
        pltpu.make_async_copy(g_hbm.at[pl.ds(mode * modes, modes)], g_all, local_sem.at[0]),
        pltpu.make_async_copy(gm_hbm.at[pl.ds(mode * modes, modes)], gm_all, local_sem.at[1]),
        pltpu.make_async_copy(x_hbm, x_all.at[chaos], local_sem.at[2]),
    ]
    for k in range(modes):
        for s in range(slots):
            locals_.append(pltpu.make_async_copy(
                t_hbm.at[k, :, s],
                t_all.at[:, pl.ds(k * blk, blk), pl.ds(s * blk, blk)],
                local_sem.at[3 + k * slots + s],
            ))

    barrier = pltpu.get_barrier_semaphore()
    for d in range(1, n):
        pl.semaphore_signal(barrier, inc=1, device_id={"chaos": lax.rem(chaos + d, n)}, device_id_type=MESH)
    pl.semaphore_signal(barrier, inc=1, device_id={"mode": other}, device_id_type=MESH)
    pl.semaphore_signal(barrier, inc=1, device_id={"space": above}, device_id_type=MESH)
    pl.semaphore_signal(barrier, inc=1, device_id={"space": below}, device_id_type=MESH)
    for copy in locals_:
        copy.start()
    pl.semaphore_wait(barrier, n + 2)

    def first_row(i):
        return lax.rem(2 * i + block_rows - 2, block_rows)

    def send_x(i, d):
        cols = pl.ds(pl.multiple_of((first_row(i) + mode) * blk, blk), blk)
        return pltpu.make_async_remote_copy(
            src_ref=x_hbm.at[:, cols], dst_ref=x_all.at[chaos, :, cols],
            send_sem=xs.at[d - 1, i], recv_sem=xr.at[d - 1, i],
            device_id={"chaos": lax.rem(chaos + d, n)}, device_id_type=MESH)

    def got_x(i, d):
        source = lax.rem(chaos + n - d, n)
        cols = pl.ds(pl.multiple_of((first_row(i) + mode) * blk, blk), blk)
        return pltpu.make_async_remote_copy(
            src_ref=x_hbm.at[:, cols], dst_ref=x_all.at[source, :, cols],
            send_sem=xs.at[d - 1, i], recv_sem=xr.at[d - 1, i],
            device_id={"chaos": lax.rem(chaos + d, n)}, device_id_type=MESH)

    def forward(i, d, which):
        source = lax.rem(chaos + n - d, n)
        cols = pl.ds(pl.multiple_of((first_row(i) + which) * blk, blk), blk)
        return pltpu.make_async_remote_copy(
            src_ref=x_all.at[source, :, cols], dst_ref=x_all.at[source, :, cols],
            send_sem=fs.at[d - 1, i], recv_sem=fr.at[d - 1, i],
            device_id={"mode": other}, device_id_type=MESH)

    def first_column(q):
        return lax.rem(2 * q + span - 2, span)

    def exchange(q):
        at = pl.ds(first_column(q), 2)
        return pltpu.make_async_remote_copy(
            src_ref=part.at[at, pl.ds(rows, rows)], dst_ref=recv.at[at],
            send_sem=ys.at[q], recv_sem=yr.at[q],
            device_id={"mode": other}, device_id_type=MESH)

    def send_rim(q):
        return pltpu.make_async_remote_copy(
            src_ref=rim.at[q], dst_ref=halo.at[q],
            send_sem=hs.at[q], recv_sem=hr.at[q],
            device_id={"space": above if q == 0 else below}, device_id_type=MESH)

    def start_x(i, carry):
        for d in range(1, n):
            send_x(i, d).start()
        return carry

    lax.fori_loop(0, chunks, start_x, 0)

    locals_[0].wait()
    locals_[1].wait()
    size_r = 2 * group * own_p
    half = half_ref[...]
    target = (2 * chaos + half * (1 - 2 * mode) + mode) * own_p + place_ref[...]
    pick = (lax.broadcasted_iota(jnp.int32, (size_r, p_size), 1) == target).astype(F32).astype(BF16)
    nt = (((1,), (1,)), ((), ()))
    for k in range(modes):
        first = lax.broadcasted_iota(jnp.int32, (p_size, p_size), 0)
        second = lax.broadcasted_iota(jnp.int32, (p_size, p_size), 1)
        value = jnp.where((first == second) | (gm_all[k] == 1), g_all[k], 0.0)
        hi = value.astype(BF16)
        lo = (value - hi.astype(F32)).astype(BF16)
        hi = lax.dot_general(pick, hi, nt, preferred_element_type=F32).astype(BF16)
        lo = lax.dot_general(pick, lo, nt, preferred_element_type=F32).astype(BF16)
        both = (jnp.dot(hi, spread_ref[0], preferred_element_type=F32)
                + jnp.dot(lo, spread_ref[1], preferred_element_type=F32))
        mix[pl.ds(k * size_r, size_r), :] = (both * same_ref[...]).astype(BF16)
    contrib[zero_at] = jnp.zeros((2 * rows, blk), F32)
    for copy in locals_[2:]:
        copy.wait()

    def compute(i):
        r0 = first_row(i)
        cols = pl.ds(pl.multiple_of(r0 * blk, 2 * blk), 2 * blk)
        operator = mix[...]
        pieces = []
        for g in range(fields // group):
            at = pl.ds(g * group * rows_in, group * rows_in)
            x = [x_all[s, at, cols] for s in range(n)]
            pieces.append(jnp.dot(operator, jnp.concatenate(x + x, axis=0), preferred_element_type=F32))
        part_rows = group * own_p
        for k in range(modes):
            value = jnp.concatenate([
                piece[k * size_r + h * part_rows:k * size_r + (h + 1) * part_rows]
                for h in range(2) for piece in pieces], axis=0)
            hi = value.astype(BF16)
            lo = (value - hi.astype(F32)).astype(BF16)
            for b in range(2):
                z[b, 0:2 * rows, k * blk:(k + 1) * blk] = hi[:, b * blk:(b + 1) * blk]
                z[b, 2 * rows:4 * rows, k * blk:(k + 1) * blk] = lo[:, b * blk:(b + 1) * blk]
        for b in range(2):
            res = jnp.dot(z[b], t_all[r0 + b], preferred_element_type=F32)
            res = res[:2 * rows] + res[2 * rows:]
            for s in range(slots):
                contrib[(r0 + b) * slots + s] = res[:, s * blk:(s + 1) * blk]

    def combine(q):
        j0 = first_column(q)
        for e in range(2):
            column = j0 + e - REACH
            total = None
            for o in range(-REACH, REACH + 1):
                r = column - o
                inside = (r >= 0) & (r < block_rows)
                rc = jnp.clip(r, 0, block_rows - 1)
                if o == 0:
                    found = rc * slots
                else:
                    found = zero_at
                    for s in range(1, slots):
                        offset = lax.rem(cols_ref[rc, s] - (space * block_rows + rc) + shell + REACH, shell) - REACH
                        found = jnp.where(offset == o, rc * slots + s, found)
                term = contrib[jnp.where(inside, found, zero_at)]
                total = term if total is None else total + term
            part[j0 + e] = total
        exchange(q).start()

    def summed(j):
        return part[j, 0:rows] + recv[j]

    def store(column, value):
        value = jnp.dot(perm_ref[...], value.astype(BF16), preferred_element_type=F32)
        start = column * blk
        if not isinstance(start, int):
            start = pl.multiple_of(start, blk)
        out_ref[:, pl.ds(start, blk)] = value.astype(BF16)

    def finish(q):
        exchange(q).wait()
        j0 = first_column(q)
        for e in range(2):
            store(j0 + e - REACH, summed(j0 + e))

    def finish_rim(q):
        exchange(q).wait()
        j0 = (2 * q + span - 2) % span
        for e in range(2):
            rim[q, e] = summed(j0 + e)
        send_rim(q).start()

    def step(t, carry):
        @pl.when(t < chunks)
        def _():
            for d in range(1, n):
                got_x(t, d).wait_recv()
                forward(t, d, mode).start()

        @pl.when(t >= 1)
        def _():
            for d in range(1, n):
                forward(t - 1, d, other).wait_recv()
            compute(t - 1)
            combine(t - 1)

        @pl.when(t == 2)
        def _():
            finish_rim(0)

        @pl.when(t == 3)
        def _():
            finish_rim(1)

        @pl.when(t >= 5)
        def _():
            finish(t - 2)
        return carry

    lax.fori_loop(0, chunks + 1, step, 0)
    combine(chunks)
    combine(chunks + 1)
    for q in range(chunks - 1, chunks + 1):
        finish(q)
    exchange(2).wait()
    send_rim(0).wait()
    for e in range(2):
        store(e, summed(REACH + e) + halo[0, e])
    exchange(chunks + 1).wait()
    send_rim(1).wait()
    for e in range(2):
        store(block_rows - 2 + e, summed(block_rows + e) + halo[1, e])

    def drain(i, carry):
        for d in range(1, n):
            send_x(i, d).wait_send()
            forward(i, d, mode).wait_send()
        return carry

    lax.fori_loop(0, chunks, drain, 0)


def per_device(n, space_size, coeffs, tangent, block_cols, galerkin, galerkin_mask):
    fields, rows_in, tile = coeffs.shape
    modes, block_rows, slots, blk, _ = tangent.shape
    p_size = galerkin.shape[1]
    own_p = p_size // (2 * n)
    group = group_of(fields, rows_in, own_p)
    rows = fields * own_p
    width = n * group * rows_in
    span = block_rows + 2 * REACH
    chunks = block_rows // 2
    size_r = 2 * group * own_p

    src, fld, q = np.meshgrid(np.arange(n), np.arange(group), np.arange(rows_in), indexing="ij")
    q_of = (src * rows_in + q).reshape(-1)
    one = (np.arange(p_size)[:, None] == q_of[None, :]).astype(np.float32)
    nil = np.zeros_like(one)
    spread = jnp.asarray(np.stack([np.concatenate([one, nil], 1), np.concatenate([nil, one], 1)]), BF16)
    h_of, f_of, p_of = (a.reshape(-1) for a in np.meshgrid(np.arange(2), np.arange(group), np.arange(own_p), indexing="ij"))
    same = jnp.asarray((f_of[:, None] == np.tile(fld.reshape(-1), 2)[None, :]).astype(np.float32))
    half = jnp.asarray(np.repeat(h_of[:, None], p_size, 1).astype(np.int32))
    place = jnp.asarray(np.repeat(p_of[:, None], p_size, 1).astype(np.int32))
    to = np.arange(rows)
    source = (to % fields) * own_p + to // fields
    perm = jnp.asarray((source[:, None] == np.arange(rows)[None, :]).astype(np.float32), BF16)

    dims = (n, space_size, fields, rows_in, own_p, group, modes, block_rows, slots, blk)
    any_ = pl.BlockSpec(memory_space=pl.ANY)
    vmem = pl.BlockSpec(memory_space=pltpu.VMEM)
    out = pl.pallas_call(
        functools.partial(kernel, dims),
        out_shape=jax.ShapeDtypeStruct((rows, tile), BF16),
        in_specs=[pl.BlockSpec(memory_space=pltpu.SMEM), any_, any_, any_, any_, vmem, vmem, vmem, vmem, vmem],
        out_specs=vmem,
        scratch_shapes=[
            pltpu.VMEM((n, fields * rows_in, tile), BF16),
            pltpu.VMEM((block_rows, modes * blk, slots * blk), BF16),
            pltpu.VMEM((modes, p_size, p_size), F32),
            pltpu.VMEM((modes, p_size, p_size), jnp.int32),
            pltpu.VMEM((modes * size_r, 2 * width), BF16),
            pltpu.VMEM((2, 4 * rows, modes * blk), BF16),
            pltpu.VMEM((block_rows * slots + 1, 2 * rows, blk), F32),
            pltpu.VMEM((span, 2 * rows, blk), F32),
            pltpu.VMEM((span, rows, blk), F32),
            pltpu.VMEM((2, REACH, rows, blk), F32),
            pltpu.VMEM((2, REACH, rows, blk), F32),
            pltpu.SemaphoreType.DMA((3 + modes * slots,)),
            pltpu.SemaphoreType.DMA((n - 1, chunks)),
            pltpu.SemaphoreType.DMA((n - 1, chunks)),
            pltpu.SemaphoreType.DMA((n - 1, chunks)),
            pltpu.SemaphoreType.DMA((n - 1, chunks)),
            pltpu.SemaphoreType.DMA((chunks + 2,)),
            pltpu.SemaphoreType.DMA((chunks + 2,)),
            pltpu.SemaphoreType.DMA((2,)),
            pltpu.SemaphoreType.DMA((2,)),
        ],
        compiler_params=pltpu.CompilerParams(
            collective_id=0, has_side_effects=True, vmem_limit_bytes=48 * 1024 * 1024),
    )(block_cols, coeffs.reshape(fields * rows_in, tile), tangent, galerkin, galerkin_mask,
      spread, same, half, place, perm)
    return jnp.transpose(out.reshape(own_p, fields, tile), (1, 0, 2))


def solution(mesh):
    return jax.shard_map(
        functools.partial(per_device, mesh.shape["chaos"], mesh.shape["space"]),
        mesh=mesh,
        in_specs=(
            P(None, "chaos", ("grp", "space")),
            P("mode", ("grp", "space"), None, None, None),
            P(("grp", "space"), None),
            P(),
            P(),
        ),
        out_specs=P(None, ("chaos", "mode"), ("grp", "space")),
        check_vma=False,
    )
```

```python
import functools

import jax
import jax.numpy as jnp
import numpy as np
from jax import lax
from jax.experimental import pallas as pl
from jax.experimental.pallas import tpu as pltpu
from jax.sharding import PartitionSpec as P

REACH = 2
MESH = pl.DeviceIdType.MESH
F32 = jnp.float32
BF16 = jnp.bfloat16


def group_of(fields, rows_in, own_p):
    for group in range(1, fields + 1):
        if fields % group == 0 and group * rows_in % 16 == 0 and group * own_p % 8 == 0:
            return group
    return fields


def kernel(dims, cols_hbm, x_hbm, t_hbm, g_hbm, gm_hbm, spread_hbm, same_hbm, half_hbm, place_hbm, perm_hbm,
           out_ref, cols_ref, spread_ref, same_ref, half_ref, place_ref, perm_ref, x_all, t_all, g_all, gm_all, mix, z, contrib, part, recv, rim, halo,
           local_sem, xs, xr, fs, fr, ys, yr, hs, hr):
    n, space_size, fields, rows_in, own_p, group, modes, block_rows, slots, blk = dims
    chaos = lax.axis_index("chaos")
    mode = lax.axis_index("mode")
    space = lax.axis_index("space")
    other = 1 - mode
    above = lax.rem(space + 1, space_size)
    below = lax.rem(space + space_size - 1, space_size)
    span = block_rows + 2 * REACH
    chunks = block_rows // 2
    pairs = span // 2
    rows = fields * own_p
    p_size = n * rows_in
    shell = block_rows * space_size
    zero_at = block_rows * slots

    locals_ = [
        pltpu.make_async_copy(g_hbm.at[pl.ds(mode * modes, modes)], g_all, local_sem.at[0]),
        pltpu.make_async_copy(gm_hbm.at[pl.ds(mode * modes, modes)], gm_all, local_sem.at[1]),
        pltpu.make_async_copy(spread_hbm, spread_ref, local_sem.at[2]),
        pltpu.make_async_copy(same_hbm, same_ref, local_sem.at[3]),
        pltpu.make_async_copy(half_hbm, half_ref, local_sem.at[4]),
        pltpu.make_async_copy(place_hbm, place_ref, local_sem.at[5]),
        pltpu.make_async_copy(perm_hbm, perm_ref, local_sem.at[6]),
        pltpu.make_async_copy(cols_hbm, cols_ref, local_sem.at[7]),
        pltpu.make_async_copy(x_hbm, x_all.at[chaos], local_sem.at[8]),
    ]
    for k in range(modes):
        for s in range(slots):
            locals_.append(pltpu.make_async_copy(
                t_hbm.at[k, :, s],
                t_all.at[:, pl.ds(k * blk, blk), pl.ds(s * blk, blk)],
                local_sem.at[9 + k * slots + s],
            ))

    barrier = pltpu.get_barrier_semaphore()
    for d in range(1, n):
        pl.semaphore_signal(barrier, inc=1, device_id={"chaos": lax.rem(chaos + d, n)}, device_id_type=MESH)
    pl.semaphore_signal(barrier, inc=1, device_id={"mode": other}, device_id_type=MESH)
    pl.semaphore_signal(barrier, inc=1, device_id={"space": above}, device_id_type=MESH)
    pl.semaphore_signal(barrier, inc=1, device_id={"space": below}, device_id_type=MESH)
    for copy in locals_:
        copy.start()
    pl.semaphore_wait(barrier, n + 2)

    def first_row(i):
        return lax.rem(2 * i + block_rows - 2, block_rows)

    def send_x(i, d):
        cols = pl.ds(pl.multiple_of((first_row(i) + mode) * blk, blk), blk)
        return pltpu.make_async_remote_copy(
            src_ref=x_hbm.at[:, cols], dst_ref=x_all.at[chaos, :, cols],
            send_sem=xs.at[d - 1, i], recv_sem=xr.at[d - 1, i],
            device_id={"chaos": lax.rem(chaos + d, n)}, device_id_type=MESH)

    def got_x(i, d):
        source = lax.rem(chaos + n - d, n)
        cols = pl.ds(pl.multiple_of((first_row(i) + mode) * blk, blk), blk)
        return pltpu.make_async_remote_copy(
            src_ref=x_hbm.at[:, cols], dst_ref=x_all.at[source, :, cols],
            send_sem=xs.at[d - 1, i], recv_sem=xr.at[d - 1, i],
            device_id={"chaos": lax.rem(chaos + d, n)}, device_id_type=MESH)

    def forward(i, d, which):
        source = lax.rem(chaos + n - d, n)
        cols = pl.ds(pl.multiple_of((first_row(i) + which) * blk, blk), blk)
        return pltpu.make_async_remote_copy(
            src_ref=x_all.at[source, :, cols], dst_ref=x_all.at[source, :, cols],
            send_sem=fs.at[d - 1, i], recv_sem=fr.at[d - 1, i],
            device_id={"mode": other}, device_id_type=MESH)

    def first_column(q):
        return lax.rem(2 * q + span - 2, span)

    def exchange(q):
        at = pl.ds(first_column(q), 2)
        return pltpu.make_async_remote_copy(
            src_ref=part.at[at, pl.ds(rows, rows)], dst_ref=recv.at[at],
            send_sem=ys.at[q], recv_sem=yr.at[q],
            device_id={"mode": other}, device_id_type=MESH)

    def send_rim(q):
        return pltpu.make_async_remote_copy(
            src_ref=rim.at[q], dst_ref=halo.at[q],
            send_sem=hs.at[q], recv_sem=hr.at[q],
            device_id={"space": above if q == 0 else below}, device_id_type=MESH)

    def start_x(i, carry):
        for d in range(1, n):
            send_x(i, d).start()
        return carry

    lax.fori_loop(0, chunks, start_x, 0)

    for copy in locals_[:8]:
        copy.wait()
    size_r = 2 * group * own_p
    half = half_ref[...]
    target = (2 * chaos + half * (1 - 2 * mode) + mode) * own_p + place_ref[...]
    pick = (lax.broadcasted_iota(jnp.int32, (size_r, p_size), 1) == target).astype(F32).astype(BF16)
    nt = (((1,), (1,)), ((), ()))
    for k in range(modes):
        first = lax.broadcasted_iota(jnp.int32, (p_size, p_size), 0)
        second = lax.broadcasted_iota(jnp.int32, (p_size, p_size), 1)
        value = jnp.where((first == second) | (gm_all[k] == 1), g_all[k], 0.0)
        hi = value.astype(BF16)
        lo = (value - hi.astype(F32)).astype(BF16)
        hi = lax.dot_general(pick, hi, nt, preferred_element_type=F32).astype(BF16)
        lo = lax.dot_general(pick, lo, nt, preferred_element_type=F32).astype(BF16)
        both = (jnp.dot(hi, spread_ref[0], preferred_element_type=F32)
                + jnp.dot(lo, spread_ref[1], preferred_element_type=F32))
        mix[pl.ds(k * size_r, size_r), :] = (both * same_ref[...]).astype(BF16)
    contrib[zero_at] = jnp.zeros((2 * rows, blk), F32)
    for copy in locals_[8:]:
        copy.wait()

    def compute(i):
        r0 = first_row(i)
        cols = pl.ds(pl.multiple_of(r0 * blk, 2 * blk), 2 * blk)
        operator = mix[...]
        pieces = []
        for g in range(fields // group):
            at = pl.ds(g * group * rows_in, group * rows_in)
            x = [x_all[s, at, cols] for s in range(n)]
            pieces.append(jnp.dot(operator, jnp.concatenate(x + x, axis=0), preferred_element_type=F32))
        part_rows = group * own_p
        for k in range(modes):
            value = jnp.concatenate([
                piece[k * size_r + h * part_rows:k * size_r + (h + 1) * part_rows]
                for h in range(2) for piece in pieces], axis=0)
            hi = value.astype(BF16)
            lo = (value - hi.astype(F32)).astype(BF16)
            for b in range(2):
                z[b, 0:2 * rows, k * blk:(k + 1) * blk] = hi[:, b * blk:(b + 1) * blk]
                z[b, 2 * rows:4 * rows, k * blk:(k + 1) * blk] = lo[:, b * blk:(b + 1) * blk]
        for b in range(2):
            res = jnp.dot(z[b], t_all[r0 + b], preferred_element_type=F32)
            res = res[:2 * rows] + res[2 * rows:]
            for s in range(slots):
                contrib[(r0 + b) * slots + s] = res[:, s * blk:(s + 1) * blk]

    def combine(q):
        j0 = first_column(q)
        for e in range(2):
            column = j0 + e - REACH
            total = None
            for o in range(-REACH, REACH + 1):
                r = column - o
                inside = (r >= 0) & (r < block_rows)
                rc = jnp.clip(r, 0, block_rows - 1)
                if o == 0:
                    found = rc * slots
                else:
                    found = zero_at
                    for s in range(1, slots):
                        offset = lax.rem(cols_ref[s, rc] - (space * block_rows + rc) + shell + REACH, shell) - REACH
                        found = jnp.where(offset == o, rc * slots + s, found)
                term = contrib[jnp.where(inside, found, zero_at)]
                total = term if total is None else total + term
            part[j0 + e] = total
        exchange(q).start()

    def summed(j):
        return part[j, 0:rows] + recv[j]

    def store(column, value):
        value = jnp.dot(perm_ref[...], value.astype(BF16), preferred_element_type=F32)
        start = column * blk
        if not isinstance(start, int):
            start = pl.multiple_of(start, blk)
        out_ref[:, pl.ds(start, blk)] = value.astype(BF16)

    def finish(q):
        exchange(q).wait()
        j0 = first_column(q)
        for e in range(2):
            store(j0 + e - REACH, summed(j0 + e))

    def finish_rim(q):
        exchange(q).wait()
        j0 = (2 * q + span - 2) % span
        for e in range(2):
            rim[q, e] = summed(j0 + e)
        send_rim(q).start()

    def step(t, carry):
        @pl.when(t < chunks)
        def _():
            for d in range(1, n):
                got_x(t, d).wait_recv()
                forward(t, d, mode).start()

        @pl.when(t >= 1)
        def _():
            for d in range(1, n):
                forward(t - 1, d, other).wait_recv()
            compute(t - 1)
            combine(t - 1)

        @pl.when(t == 2)
        def _():
            finish_rim(0)

        @pl.when(t == 3)
        def _():
            finish_rim(1)

        @pl.when(t >= 5)
        def _():
            finish(t - 2)
        return carry

    lax.fori_loop(0, chunks + 1, step, 0)
    combine(chunks)
    combine(chunks + 1)
    for q in range(chunks - 1, chunks + 1):
        finish(q)
    exchange(2).wait()
    send_rim(0).wait()
    for e in range(2):
        store(e, summed(REACH + e) + halo[0, e])
    exchange(chunks + 1).wait()
    send_rim(1).wait()
    for e in range(2):
        store(block_rows - 2 + e, summed(block_rows + e) + halo[1, e])

    def drain(i, carry):
        for d in range(1, n):
            send_x(i, d).wait_send()
            forward(i, d, mode).wait_send()
        return carry

    lax.fori_loop(0, chunks, drain, 0)


def per_device(n, space_size, coeffs, tangent, block_cols, galerkin, galerkin_mask):
    fields, rows_in, tile = coeffs.shape
    modes, block_rows, slots, blk, _ = tangent.shape
    p_size = galerkin.shape[1]
    own_p = p_size // (2 * n)
    group = group_of(fields, rows_in, own_p)
    rows = fields * own_p
    width = n * group * rows_in
    span = block_rows + 2 * REACH
    chunks = block_rows // 2
    size_r = 2 * group * own_p

    src, fld, q = np.meshgrid(np.arange(n), np.arange(group), np.arange(rows_in), indexing="ij")
    q_of = (src * rows_in + q).reshape(-1)
    one = (np.arange(p_size)[:, None] == q_of[None, :]).astype(np.float32)
    nil = np.zeros_like(one)
    spread = jnp.asarray(np.stack([np.concatenate([one, nil], 1), np.concatenate([nil, one], 1)]), BF16)
    h_of, f_of, p_of = (a.reshape(-1) for a in np.meshgrid(np.arange(2), np.arange(group), np.arange(own_p), indexing="ij"))
    same = jnp.asarray((f_of[:, None] == np.tile(fld.reshape(-1), 2)[None, :]).astype(np.float32))
    half = jnp.asarray(np.repeat(h_of[:, None], p_size, 1).astype(np.int32))
    place = jnp.asarray(np.repeat(p_of[:, None], p_size, 1).astype(np.int32))
    to = np.arange(rows)
    source = (to % fields) * own_p + to // fields
    perm = jnp.asarray((source[:, None] == np.arange(rows)[None, :]).astype(np.float32), BF16)

    dims = (n, space_size, fields, rows_in, own_p, group, modes, block_rows, slots, blk)
    hbm = pl.BlockSpec(memory_space=pltpu.HBM)
    vmem = pl.BlockSpec(memory_space=pltpu.VMEM)
    out = pl.pallas_call(
        functools.partial(kernel, dims),
        out_shape=jax.ShapeDtypeStruct((rows, tile), BF16),
        in_specs=[hbm] * 10,
        out_specs=vmem,
        scratch_shapes=[
            pltpu.SMEM((slots, block_rows), jnp.int32),
            pltpu.VMEM(spread.shape, BF16),
            pltpu.VMEM(same.shape, F32),
            pltpu.VMEM(half.shape, jnp.int32),
            pltpu.VMEM(place.shape, jnp.int32),
            pltpu.VMEM(perm.shape, BF16),
            pltpu.VMEM((n, fields * rows_in, tile), BF16),
            pltpu.VMEM((block_rows, modes * blk, slots * blk), BF16),
            pltpu.VMEM((modes, p_size, p_size), F32),
            pltpu.VMEM((modes, p_size, p_size), jnp.int32),
            pltpu.VMEM((modes * size_r, 2 * width), BF16),
            pltpu.VMEM((2, 4 * rows, modes * blk), BF16),
            pltpu.VMEM((block_rows * slots + 1, 2 * rows, blk), F32),
            pltpu.VMEM((span, 2 * rows, blk), F32),
            pltpu.VMEM((span, rows, blk), F32),
            pltpu.VMEM((2, REACH, rows, blk), F32),
            pltpu.VMEM((2, REACH, rows, blk), F32),
            pltpu.SemaphoreType.DMA((9 + modes * slots,)),
            pltpu.SemaphoreType.DMA((n - 1, chunks)),
            pltpu.SemaphoreType.DMA((n - 1, chunks)),
            pltpu.SemaphoreType.DMA((n - 1, chunks)),
            pltpu.SemaphoreType.DMA((n - 1, chunks)),
            pltpu.SemaphoreType.DMA((chunks + 2,)),
            pltpu.SemaphoreType.DMA((chunks + 2,)),
            pltpu.SemaphoreType.DMA((2,)),
            pltpu.SemaphoreType.DMA((2,)),
        ],
        compiler_params=pltpu.CompilerParams(
            collective_id=0, has_side_effects=True, vmem_limit_bytes=60 * 1024 * 1024),
    )(block_cols.T, coeffs.reshape(fields * rows_in, tile), tangent, galerkin, galerkin_mask,
      spread, same, half, place, perm)
    return jnp.transpose(out.reshape(own_p, fields, tile), (1, 0, 2))


def solution(mesh):
    return jax.shard_map(
        functools.partial(per_device, mesh.shape["chaos"], mesh.shape["space"]),
        mesh=mesh,
        in_specs=(
            P(None, "chaos", ("grp", "space")),
            P("mode", ("grp", "space"), None, None, None),
            P(("grp", "space"), None),
            P(),
            P(),
        ),
        out_specs=P(None, ("chaos", "mode"), ("grp", "space")),
        check_vma=False,
    )
```

```python
import functools

import jax
import jax.numpy as jnp
import numpy as np
from jax import lax
from jax.experimental import pallas as pl
from jax.experimental.pallas import tpu as pltpu
from jax.sharding import PartitionSpec as P

REACH = 2
MESH = pl.DeviceIdType.MESH
F32 = jnp.float32
BF16 = jnp.bfloat16


def group_of(fields, rows_in, own_p):
    for group in range(1, fields + 1):
        if fields % group == 0 and group * rows_in % 16 == 0 and group * own_p % 8 == 0:
            return group
    return fields


def kernel(dims, cols_hbm, x_hbm, t_hbm, g_hbm, gm_hbm, spread_hbm, same_hbm, half_hbm, place_hbm, perm_hbm,
           out_ref, cols_ref, spread_ref, same_ref, half_ref, place_ref, perm_ref, x_all, t_all, g_all, gm_all, mix, z, contrib, part, recv, rim, halo,
           local_sem, xs, xr, fs, fr, ys, yr, hs, hr):
    n, space_size, fields, rows_in, own_p, group, modes, block_rows, slots, blk = dims
    chaos = lax.axis_index("chaos")
    mode = lax.axis_index("mode")
    space = lax.axis_index("space")
    other = 1 - mode
    above = lax.rem(space + 1, space_size)
    below = lax.rem(space + space_size - 1, space_size)
    span = block_rows + 2 * REACH
    chunks = block_rows // 2
    pairs = span // 2
    rows = fields * own_p
    p_size = n * rows_in
    shell = block_rows * space_size
    zero_at = block_rows * slots

    locals_ = [
        pltpu.make_async_copy(g_hbm.at[pl.ds(mode * modes, modes)], g_all, local_sem.at[0]),
        pltpu.make_async_copy(gm_hbm.at[pl.ds(mode * modes, modes)], gm_all, local_sem.at[1]),
        pltpu.make_async_copy(spread_hbm, spread_ref, local_sem.at[2]),
        pltpu.make_async_copy(same_hbm, same_ref, local_sem.at[3]),
        pltpu.make_async_copy(half_hbm, half_ref, local_sem.at[4]),
        pltpu.make_async_copy(place_hbm, place_ref, local_sem.at[5]),
        pltpu.make_async_copy(perm_hbm, perm_ref, local_sem.at[6]),
        pltpu.make_async_copy(cols_hbm, cols_ref, local_sem.at[7]),
        pltpu.make_async_copy(x_hbm, x_all.at[chaos], local_sem.at[8]),
    ]
    for k in range(modes):
        locals_.append(pltpu.make_async_copy(
            t_hbm.at[k], t_all.at[:, :, pl.ds(k * blk, blk)], local_sem.at[9 + k]))

    barrier = pltpu.get_barrier_semaphore()
    for d in range(1, n):
        pl.semaphore_signal(barrier, inc=1, device_id={"chaos": lax.rem(chaos + d, n)}, device_id_type=MESH)
    pl.semaphore_signal(barrier, inc=1, device_id={"mode": other}, device_id_type=MESH)
    pl.semaphore_signal(barrier, inc=1, device_id={"space": above}, device_id_type=MESH)
    pl.semaphore_signal(barrier, inc=1, device_id={"space": below}, device_id_type=MESH)
    for copy in locals_:
        copy.start()
    pl.semaphore_wait(barrier, n + 2)

    def first_row(i):
        return lax.rem(2 * i + block_rows - 2, block_rows)

    def send_x(i, d):
        cols = pl.ds(pl.multiple_of((first_row(i) + mode) * blk, blk), blk)
        return pltpu.make_async_remote_copy(
            src_ref=x_hbm.at[:, cols], dst_ref=x_all.at[chaos, :, cols],
            send_sem=xs.at[d - 1, i], recv_sem=xr.at[d - 1, i],
            device_id={"chaos": lax.rem(chaos + d, n)}, device_id_type=MESH)

    def got_x(i, d):
        source = lax.rem(chaos + n - d, n)
        cols = pl.ds(pl.multiple_of((first_row(i) + mode) * blk, blk), blk)
        return pltpu.make_async_remote_copy(
            src_ref=x_hbm.at[:, cols], dst_ref=x_all.at[source, :, cols],
            send_sem=xs.at[d - 1, i], recv_sem=xr.at[d - 1, i],
            device_id={"chaos": lax.rem(chaos + d, n)}, device_id_type=MESH)

    def forward(i, d, which):
        source = lax.rem(chaos + n - d, n)
        cols = pl.ds(pl.multiple_of((first_row(i) + which) * blk, blk), blk)
        return pltpu.make_async_remote_copy(
            src_ref=x_all.at[source, :, cols], dst_ref=x_all.at[source, :, cols],
            send_sem=fs.at[d - 1, i], recv_sem=fr.at[d - 1, i],
            device_id={"mode": other}, device_id_type=MESH)

    def first_column(q):
        return lax.rem(2 * q + span - 2, span)

    def exchange(q):
        at = pl.ds(first_column(q), 2)
        return pltpu.make_async_remote_copy(
            src_ref=part.at[at, pl.ds(rows, rows)], dst_ref=recv.at[at],
            send_sem=ys.at[q], recv_sem=yr.at[q],
            device_id={"mode": other}, device_id_type=MESH)

    def send_rim(q):
        return pltpu.make_async_remote_copy(
            src_ref=rim.at[q], dst_ref=halo.at[q],
            send_sem=hs.at[q], recv_sem=hr.at[q],
            device_id={"space": above if q == 0 else below}, device_id_type=MESH)

    def start_x(i, carry):
        for d in range(1, n):
            send_x(i, d).start()
        return carry

    lax.fori_loop(0, chunks, start_x, 0)

    for copy in locals_[:8]:
        copy.wait()
    size_r = 2 * group * own_p
    half = half_ref[...]
    target = (2 * chaos + half * (1 - 2 * mode) + mode) * own_p + place_ref[...]
    pick = (lax.broadcasted_iota(jnp.int32, (size_r, p_size), 1) == target).astype(F32).astype(BF16)
    nt = (((1,), (1,)), ((), ()))
    for k in range(modes):
        first = lax.broadcasted_iota(jnp.int32, (p_size, p_size), 0)
        second = lax.broadcasted_iota(jnp.int32, (p_size, p_size), 1)
        value = jnp.where((first == second) | (gm_all[k] == 1), g_all[k], 0.0)
        hi = value.astype(BF16)
        lo = (value - hi.astype(F32)).astype(BF16)
        hi = lax.dot_general(pick, hi, nt, preferred_element_type=F32).astype(BF16)
        lo = lax.dot_general(pick, lo, nt, preferred_element_type=F32).astype(BF16)
        both = (jnp.dot(hi, spread_ref[0], preferred_element_type=F32)
                + jnp.dot(lo, spread_ref[1], preferred_element_type=F32))
        mix[pl.ds(k * size_r, size_r), :] = (both * same_ref[...]).astype(BF16)
    contrib[zero_at] = jnp.zeros((2 * rows, blk), F32)
    for copy in locals_[8:]:
        copy.wait()

    def compute(i):
        r0 = first_row(i)
        cols = pl.ds(pl.multiple_of(r0 * blk, 2 * blk), 2 * blk)
        operator = mix[...]
        pieces = []
        for g in range(fields // group):
            at = pl.ds(g * group * rows_in, group * rows_in)
            x = [x_all[s, at, cols] for s in range(n)]
            pieces.append(jnp.dot(operator, jnp.concatenate(x + x, axis=0), preferred_element_type=F32))
        part_rows = group * own_p
        for k in range(modes):
            value = jnp.concatenate([
                piece[k * size_r + h * part_rows:k * size_r + (h + 1) * part_rows]
                for h in range(2) for piece in pieces], axis=0)
            hi = value.astype(BF16)
            lo = (value - hi.astype(F32)).astype(BF16)
            for b in range(2):
                z[b, 0:2 * rows, k * blk:(k + 1) * blk] = hi[:, b * blk:(b + 1) * blk]
                z[b, 2 * rows:4 * rows, k * blk:(k + 1) * blk] = lo[:, b * blk:(b + 1) * blk]
        for b in range(2):
            right = jnp.concatenate([t_all[r0 + b, s] for s in range(slots)], axis=1)
            res = jnp.dot(z[b], right, preferred_element_type=F32)
            res = res[:2 * rows] + res[2 * rows:]
            for s in range(slots):
                contrib[(r0 + b) * slots + s] = res[:, s * blk:(s + 1) * blk]

    def combine(q):
        j0 = first_column(q)
        for e in range(2):
            column = j0 + e - REACH
            total = None
            for o in range(-REACH, REACH + 1):
                r = column - o
                inside = (r >= 0) & (r < block_rows)
                rc = jnp.clip(r, 0, block_rows - 1)
                if o == 0:
                    found = rc * slots
                else:
                    found = zero_at
                    for s in range(1, slots):
                        offset = lax.rem(cols_ref[s, rc] - (space * block_rows + rc) + shell + REACH, shell) - REACH
                        found = jnp.where(offset == o, rc * slots + s, found)
                term = contrib[jnp.where(inside, found, zero_at)]
                total = term if total is None else total + term
            part[j0 + e] = total
        exchange(q).start()

    def summed(j):
        return part[j, 0:rows] + recv[j]

    def store(column, value):
        value = jnp.dot(perm_ref[...], value.astype(BF16), preferred_element_type=F32)
        start = column * blk
        if not isinstance(start, int):
            start = pl.multiple_of(start, blk)
        out_ref[:, pl.ds(start, blk)] = value.astype(BF16)

    def finish(q):
        exchange(q).wait()
        j0 = first_column(q)
        for e in range(2):
            store(j0 + e - REACH, summed(j0 + e))

    def finish_rim(q):
        exchange(q).wait()
        j0 = (2 * q + span - 2) % span
        for e in range(2):
            rim[q, e] = summed(j0 + e)
        send_rim(q).start()

    def step(t, carry):
        @pl.when(t < chunks)
        def _():
            for d in range(1, n):
                got_x(t, d).wait_recv()
                forward(t, d, mode).start()

        @pl.when(t >= 1)
        def _():
            for d in range(1, n):
                forward(t - 1, d, other).wait_recv()
            compute(t - 1)
            combine(t - 1)

        @pl.when(t == 2)
        def _():
            finish_rim(0)

        @pl.when(t == 3)
        def _():
            finish_rim(1)

        @pl.when(t >= 5)
        def _():
            finish(t - 2)
        return carry

    lax.fori_loop(0, chunks + 1, step, 0)
    combine(chunks)
    combine(chunks + 1)
    for q in range(chunks - 1, chunks + 1):
        finish(q)
    exchange(2).wait()
    send_rim(0).wait()
    for e in range(2):
        store(e, summed(REACH + e) + halo[0, e])
    exchange(chunks + 1).wait()
    send_rim(1).wait()
    for e in range(2):
        store(block_rows - 2 + e, summed(block_rows + e) + halo[1, e])

    def drain(i, carry):
        for d in range(1, n):
            send_x(i, d).wait_send()
            forward(i, d, mode).wait_send()
        return carry

    lax.fori_loop(0, chunks, drain, 0)


def per_device(n, space_size, coeffs, tangent, block_cols, galerkin, galerkin_mask):
    fields, rows_in, tile = coeffs.shape
    modes, block_rows, slots, blk, _ = tangent.shape
    p_size = galerkin.shape[1]
    own_p = p_size // (2 * n)
    group = group_of(fields, rows_in, own_p)
    rows = fields * own_p
    width = n * group * rows_in
    span = block_rows + 2 * REACH
    chunks = block_rows // 2
    size_r = 2 * group * own_p

    src, fld, q = np.meshgrid(np.arange(n), np.arange(group), np.arange(rows_in), indexing="ij")
    q_of = (src * rows_in + q).reshape(-1)
    one = (np.arange(p_size)[:, None] == q_of[None, :]).astype(np.float32)
    nil = np.zeros_like(one)
    spread = jnp.asarray(np.stack([np.concatenate([one, nil], 1), np.concatenate([nil, one], 1)]), BF16)
    h_of, f_of, p_of = (a.reshape(-1) for a in np.meshgrid(np.arange(2), np.arange(group), np.arange(own_p), indexing="ij"))
    same = jnp.asarray((f_of[:, None] == np.tile(fld.reshape(-1), 2)[None, :]).astype(np.float32))
    half = jnp.asarray(np.repeat(h_of[:, None], p_size, 1).astype(np.int32))
    place = jnp.asarray(np.repeat(p_of[:, None], p_size, 1).astype(np.int32))
    to = np.arange(rows)
    source = (to % fields) * own_p + to // fields
    perm = jnp.asarray((source[:, None] == np.arange(rows)[None, :]).astype(np.float32), BF16)

    dims = (n, space_size, fields, rows_in, own_p, group, modes, block_rows, slots, blk)
    hbm = pl.BlockSpec(memory_space=pltpu.HBM)
    out = pl.pallas_call(
        functools.partial(kernel, dims),
        out_shape=pltpu.VMEM((rows, tile), BF16),
        in_specs=[hbm] * 10,
        scratch_shapes=[
            pltpu.SMEM((slots, block_rows), jnp.int32),
            pltpu.VMEM(spread.shape, BF16),
            pltpu.VMEM(same.shape, F32),
            pltpu.VMEM(half.shape, jnp.int32),
            pltpu.VMEM(place.shape, jnp.int32),
            pltpu.VMEM(perm.shape, BF16),
            pltpu.VMEM((n, fields * rows_in, tile), BF16),
            pltpu.VMEM((block_rows, slots, modes * blk, blk), BF16),
            pltpu.VMEM((modes, p_size, p_size), F32),
            pltpu.VMEM((modes, p_size, p_size), jnp.int32),
            pltpu.VMEM((modes * size_r, 2 * width), BF16),
            pltpu.VMEM((2, 4 * rows, modes * blk), BF16),
            pltpu.VMEM((block_rows * slots + 1, 2 * rows, blk), F32),
            pltpu.VMEM((span, 2 * rows, blk), F32),
            pltpu.VMEM((span, rows, blk), F32),
            pltpu.VMEM((2, REACH, rows, blk), F32),
            pltpu.VMEM((2, REACH, rows, blk), F32),
            pltpu.SemaphoreType.DMA((9 + modes,)),
            pltpu.SemaphoreType.DMA((n - 1, chunks)),
            pltpu.SemaphoreType.DMA((n - 1, chunks)),
            pltpu.SemaphoreType.DMA((n - 1, chunks)),
            pltpu.SemaphoreType.DMA((n - 1, chunks)),
            pltpu.SemaphoreType.DMA((chunks + 2,)),
            pltpu.SemaphoreType.DMA((chunks + 2,)),
            pltpu.SemaphoreType.DMA((2,)),
            pltpu.SemaphoreType.DMA((2,)),
        ],
        compiler_params=pltpu.CompilerParams(
            collective_id=0, has_side_effects=True, vmem_limit_bytes=60 * 1024 * 1024),
    )(block_cols.T, coeffs.reshape(fields * rows_in, tile), tangent, galerkin, galerkin_mask,
      spread, same, half, place, perm)
    return jnp.transpose(out.reshape(own_p, fields, tile), (1, 0, 2))


def solution(mesh):
    return jax.shard_map(
        functools.partial(per_device, mesh.shape["chaos"], mesh.shape["space"]),
        mesh=mesh,
        in_specs=(
            P(None, "chaos", ("grp", "space")),
            P("mode", ("grp", "space"), None, None, None),
            P(("grp", "space"), None),
            P(),
            P(),
        ),
        out_specs=P(None, ("chaos", "mode"), ("grp", "space")),
        check_vma=False,
    )
```

```python
import functools

import jax
import jax.numpy as jnp
import numpy as np
from jax import lax
from jax.experimental import pallas as pl
from jax.experimental.pallas import tpu as pltpu
from jax.sharding import PartitionSpec as P

REACH = 2
MESH = pl.DeviceIdType.MESH
F32 = jnp.float32
BF16 = jnp.bfloat16


def group_of(fields, rows_in, own_p):
    for group in range(1, fields + 1):
        if fields % group == 0 and group * rows_in % 16 == 0 and group * own_p % 8 == 0:
            return group
    return fields


def kernel(dims, cols_hbm, x_hbm, t_hbm, g_hbm, gm_hbm, spread_hbm, same_hbm, half_hbm, place_hbm, perm_hbm,
           out_ref, cols_ref, spread_ref, same_ref, half_ref, place_ref, perm_ref, x_all, t_all, g_all, gm_all, mix, z, contrib, part, recv, rim, halo,
           local_sem, xs, xr, fs, fr, ys, yr, hs, hr):
    n, space_size, fields, rows_in, own_p, group, modes, block_rows, slots, blk = dims
    chaos = lax.axis_index("chaos")
    mode = lax.axis_index("mode")
    space = lax.axis_index("space")
    other = 1 - mode
    above = lax.rem(space + 1, space_size)
    below = lax.rem(space + space_size - 1, space_size)
    span = block_rows + 2 * REACH
    chunks = block_rows // 2
    pairs = span // 2
    rows = fields * own_p
    p_size = n * rows_in
    shell = block_rows * space_size
    zero_at = block_rows * slots

    locals_ = [
        pltpu.make_async_copy(g_hbm.at[pl.ds(mode * modes, modes)], g_all, local_sem.at[0]),
        pltpu.make_async_copy(gm_hbm.at[pl.ds(mode * modes, modes)], gm_all, local_sem.at[1]),
        pltpu.make_async_copy(spread_hbm, spread_ref, local_sem.at[2]),
        pltpu.make_async_copy(same_hbm, same_ref, local_sem.at[3]),
        pltpu.make_async_copy(half_hbm, half_ref, local_sem.at[4]),
        pltpu.make_async_copy(place_hbm, place_ref, local_sem.at[5]),
        pltpu.make_async_copy(perm_hbm, perm_ref, local_sem.at[6]),
        pltpu.make_async_copy(cols_hbm, cols_ref, local_sem.at[7]),
        pltpu.make_async_copy(x_hbm, x_all.at[chaos], local_sem.at[8]),
    ]
    for k in range(modes):
        locals_.append(pltpu.make_async_copy(
            t_hbm.at[k], t_all.at[:, :, pl.ds(k * blk, blk)], local_sem.at[9 + k]))

    barrier = pltpu.get_barrier_semaphore()
    for d in range(1, n):
        pl.semaphore_signal(barrier, inc=1, device_id={"chaos": lax.rem(chaos + d, n)}, device_id_type=MESH)
    pl.semaphore_signal(barrier, inc=1, device_id={"mode": other}, device_id_type=MESH)
    pl.semaphore_signal(barrier, inc=1, device_id={"space": above}, device_id_type=MESH)
    pl.semaphore_signal(barrier, inc=1, device_id={"space": below}, device_id_type=MESH)
    for copy in locals_:
        copy.start()
    pl.semaphore_wait(barrier, n + 2)

    def first_row(i):
        return lax.rem(2 * i + block_rows - 2, block_rows)

    def send_x(i, d):
        cols = pl.ds(pl.multiple_of((first_row(i) + mode) * blk, blk), blk)
        return pltpu.make_async_remote_copy(
            src_ref=x_hbm.at[:, cols], dst_ref=x_all.at[chaos, :, cols],
            send_sem=xs.at[d - 1, i], recv_sem=xr.at[d - 1, i],
            device_id={"chaos": lax.rem(chaos + d, n)}, device_id_type=MESH)

    def got_x(i, d):
        source = lax.rem(chaos + n - d, n)
        cols = pl.ds(pl.multiple_of((first_row(i) + mode) * blk, blk), blk)
        return pltpu.make_async_remote_copy(
            src_ref=x_hbm.at[:, cols], dst_ref=x_all.at[source, :, cols],
            send_sem=xs.at[d - 1, i], recv_sem=xr.at[d - 1, i],
            device_id={"chaos": lax.rem(chaos + d, n)}, device_id_type=MESH)

    def forward(i, d, which):
        source = lax.rem(chaos + n - d, n)
        cols = pl.ds(pl.multiple_of((first_row(i) + which) * blk, blk), blk)
        return pltpu.make_async_remote_copy(
            src_ref=x_all.at[source, :, cols], dst_ref=x_all.at[source, :, cols],
            send_sem=fs.at[d - 1, i], recv_sem=fr.at[d - 1, i],
            device_id={"mode": other}, device_id_type=MESH)

    def first_column(q):
        return lax.rem(2 * q + span - 2, span)

    def exchange(q):
        at = pl.ds(first_column(q), 2)
        return pltpu.make_async_remote_copy(
            src_ref=part.at[at, pl.ds(rows, rows)], dst_ref=recv.at[at],
            send_sem=ys.at[q], recv_sem=yr.at[q],
            device_id={"mode": other}, device_id_type=MESH)

    def send_rim(q):
        return pltpu.make_async_remote_copy(
            src_ref=rim.at[q], dst_ref=halo.at[q],
            send_sem=hs.at[q], recv_sem=hr.at[q],
            device_id={"space": above if q == 0 else below}, device_id_type=MESH)

    def start_x(i, carry):
        for d in range(1, n):
            send_x(i, d).start()
        return carry

    lax.fori_loop(0, chunks, start_x, 0)

    for copy in locals_[:8]:
        copy.wait()
    size_r = 2 * group * own_p
    half = half_ref[...]
    target = (2 * chaos + half * (1 - 2 * mode) + mode) * own_p + place_ref[...]
    pick = (lax.broadcasted_iota(jnp.int32, (size_r, p_size), 1) == target).astype(F32).astype(BF16)
    nt = (((1,), (1,)), ((), ()))
    for k in range(modes):
        first = lax.broadcasted_iota(jnp.int32, (p_size, p_size), 0)
        second = lax.broadcasted_iota(jnp.int32, (p_size, p_size), 1)
        value = jnp.where((first == second) | (gm_all[k] == 1), g_all[k], 0.0)
        hi = value.astype(BF16)
        lo = (value - hi.astype(F32)).astype(BF16)
        hi = lax.dot_general(pick, hi, nt, preferred_element_type=F32).astype(BF16)
        lo = lax.dot_general(pick, lo, nt, preferred_element_type=F32).astype(BF16)
        both = (jnp.dot(hi, spread_ref[0], preferred_element_type=F32)
                + jnp.dot(lo, spread_ref[1], preferred_element_type=F32))
        mix[pl.ds(k * size_r, size_r), :] = (both * same_ref[...]).astype(BF16)
    contrib[zero_at] = jnp.zeros((2 * rows, blk), F32)
    for copy in locals_[8:]:
        copy.wait()

    def compute(i):
        r0 = first_row(i)
        cols = pl.ds(pl.multiple_of(r0 * blk, 2 * blk), 2 * blk)
        operator = mix[...]
        pieces = []
        for g in range(fields // group):
            at = pl.ds(g * group * rows_in, group * rows_in)
            x = [x_all[s, at, cols] for s in range(n)]
            pieces.append(jnp.dot(operator, jnp.concatenate(x + x, axis=0), preferred_element_type=F32))
        part_rows = group * own_p
        for k in range(modes):
            value = jnp.concatenate([
                piece[k * size_r + h * part_rows:k * size_r + (h + 1) * part_rows]
                for h in range(2) for piece in pieces], axis=0)
            hi = value.astype(BF16)
            lo = (value - hi.astype(F32)).astype(BF16)
            for b in range(2):
                z[b, 0:2 * rows, k * blk:(k + 1) * blk] = hi[:, b * blk:(b + 1) * blk]
                z[b, 2 * rows:4 * rows, k * blk:(k + 1) * blk] = lo[:, b * blk:(b + 1) * blk]
        for b in range(2):
            right = jnp.concatenate([t_all[r0 + b, s] for s in range(slots)], axis=1)
            res = jnp.dot(z[b], right, preferred_element_type=F32)
            res = res[:2 * rows] + res[2 * rows:]
            for s in range(slots):
                contrib[(r0 + b) * slots + s] = res[:, s * blk:(s + 1) * blk]

    def combine(q):
        j0 = first_column(q)
        for e in range(2):
            column = j0 + e - REACH
            total = None
            for o in range(-REACH, REACH + 1):
                r = column - o
                inside = (r >= 0) & (r < block_rows)
                rc = jnp.clip(r, 0, block_rows - 1)
                if o == 0:
                    found = rc * slots
                else:
                    found = zero_at
                    for s in range(1, slots):
                        offset = lax.rem(cols_ref[s, rc] - (space * block_rows + rc) + shell + REACH, shell) - REACH
                        found = jnp.where(offset == o, rc * slots + s, found)
                term = contrib[jnp.where(inside, found, zero_at)]
                total = term if total is None else total + term
            part[j0 + e] = total
        exchange(q).start()

    def summed(j):
        return part[j, 0:rows] + recv[j]

    def store(column, values):
        value = jnp.concatenate([v.astype(BF16) for v in values], axis=1)
        value = jnp.dot(perm_ref[...], value, preferred_element_type=F32)
        start = column * blk
        if not isinstance(start, int):
            start = pl.multiple_of(start, 2 * blk)
        out_ref[:, pl.ds(start, 2 * blk)] = value.astype(BF16)

    def finish(q):
        exchange(q).wait()
        j0 = first_column(q)
        store(j0 - REACH, [summed(j0), summed(j0 + 1)])

    def finish_edge(q, side, column):
        exchange(q).wait()
        send_rim(side).wait()
        store(column, [summed(column + REACH + e) + halo[side, e] for e in range(2)])

    def finish_rim(q):
        exchange(q).wait()
        j0 = (2 * q + span - 2) % span
        for e in range(2):
            rim[q, e] = summed(j0 + e)
        send_rim(q).start()

    def step(t, carry):
        for d in range(1, n):
            got_x(t, d).wait_recv()
            forward(t, d, mode).start()

        @pl.when(t >= 1)
        def _():
            for d in range(1, n):
                forward(t - 1, d, other).wait_recv()
            compute(t - 1)
            combine(t - 1)

        @pl.when(t == 2)
        def _():
            finish_rim(0)

        @pl.when(t == 3)
        def _():
            finish_rim(1)

        @pl.when(t >= 5)
        def _():
            finish(t - 2)
        return carry

    lax.fori_loop(0, chunks, step, 0)
    finish_edge(2, 0, 0)
    for d in range(1, n):
        forward(chunks - 1, d, other).wait_recv()
    compute(chunks - 1)
    for q in range(chunks - 1, chunks + 2):
        combine(q)
    for q in range(chunks - 2, chunks + 1):
        finish(q)
    finish_edge(chunks + 1, 1, block_rows - 2)

    def drain(i, carry):
        for d in range(1, n):
            send_x(i, d).wait_send()
            forward(i, d, mode).wait_send()
        return carry

    lax.fori_loop(0, chunks, drain, 0)


def per_device(n, space_size, coeffs, tangent, block_cols, galerkin, galerkin_mask):
    fields, rows_in, tile = coeffs.shape
    modes, block_rows, slots, blk, _ = tangent.shape
    p_size = galerkin.shape[1]
    own_p = p_size // (2 * n)
    group = group_of(fields, rows_in, own_p)
    rows = fields * own_p
    width = n * group * rows_in
    span = block_rows + 2 * REACH
    chunks = block_rows // 2
    size_r = 2 * group * own_p

    src, fld, q = np.meshgrid(np.arange(n), np.arange(group), np.arange(rows_in), indexing="ij")
    q_of = (src * rows_in + q).reshape(-1)
    one = (np.arange(p_size)[:, None] == q_of[None, :]).astype(np.float32)
    nil = np.zeros_like(one)
    spread = jnp.asarray(np.stack([np.concatenate([one, nil], 1), np.concatenate([nil, one], 1)]), BF16)
    h_of, f_of, p_of = (a.reshape(-1) for a in np.meshgrid(np.arange(2), np.arange(group), np.arange(own_p), indexing="ij"))
    same = jnp.asarray((f_of[:, None] == np.tile(fld.reshape(-1), 2)[None, :]).astype(np.float32))
    half = jnp.asarray(np.repeat(h_of[:, None], p_size, 1).astype(np.int32))
    place = jnp.asarray(np.repeat(p_of[:, None], p_size, 1).astype(np.int32))
    to = np.arange(rows)
    source = (to % fields) * own_p + to // fields
    perm = jnp.asarray((source[:, None] == np.arange(rows)[None, :]).astype(np.float32), BF16)

    dims = (n, space_size, fields, rows_in, own_p, group, modes, block_rows, slots, blk)
    hbm = pl.BlockSpec(memory_space=pltpu.HBM)
    out = pl.pallas_call(
        functools.partial(kernel, dims),
        out_shape=pltpu.VMEM((rows, tile), BF16),
        in_specs=[hbm] * 10,
        scratch_shapes=[
            pltpu.SMEM((slots, block_rows), jnp.int32),
            pltpu.VMEM(spread.shape, BF16),
            pltpu.VMEM(same.shape, F32),
            pltpu.VMEM(half.shape, jnp.int32),
            pltpu.VMEM(place.shape, jnp.int32),
            pltpu.VMEM(perm.shape, BF16),
            pltpu.VMEM((n, fields * rows_in, tile), BF16),
            pltpu.VMEM((block_rows, slots, modes * blk, blk), BF16),
            pltpu.VMEM((modes, p_size, p_size), F32),
            pltpu.VMEM((modes, p_size, p_size), jnp.int32),
            pltpu.VMEM((modes * size_r, 2 * width), BF16),
            pltpu.VMEM((2, 4 * rows, modes * blk), BF16),
            pltpu.VMEM((block_rows * slots + 1, 2 * rows, blk), F32),
            pltpu.VMEM((span, 2 * rows, blk), F32),
            pltpu.VMEM((span, rows, blk), F32),
            pltpu.VMEM((2, REACH, rows, blk), F32),
            pltpu.VMEM((2, REACH, rows, blk), F32),
            pltpu.SemaphoreType.DMA((9 + modes,)),
            pltpu.SemaphoreType.DMA((n - 1, chunks)),
            pltpu.SemaphoreType.DMA((n - 1, chunks)),
            pltpu.SemaphoreType.DMA((n - 1, chunks)),
            pltpu.SemaphoreType.DMA((n - 1, chunks)),
            pltpu.SemaphoreType.DMA((chunks + 2,)),
            pltpu.SemaphoreType.DMA((chunks + 2,)),
            pltpu.SemaphoreType.DMA((2,)),
            pltpu.SemaphoreType.DMA((2,)),
        ],
        compiler_params=pltpu.CompilerParams(
            collective_id=0, has_side_effects=True, vmem_limit_bytes=60 * 1024 * 1024),
    )(block_cols.T, coeffs.reshape(fields * rows_in, tile), tangent, galerkin, galerkin_mask,
      spread, same, half, place, perm)
    return jnp.transpose(out.reshape(own_p, fields, tile), (1, 0, 2))


def solution(mesh):
    return jax.shard_map(
        functools.partial(per_device, mesh.shape["chaos"], mesh.shape["space"]),
        mesh=mesh,
        in_specs=(
            P(None, "chaos", ("grp", "space")),
            P("mode", ("grp", "space"), None, None, None),
            P(("grp", "space"), None),
            P(),
            P(),
        ),
        out_specs=P(None, ("chaos", "mode"), ("grp", "space")),
        check_vma=False,
    )
```

```python
import functools

import jax
import jax.numpy as jnp
import numpy as np
from jax import lax
from jax.experimental import pallas as pl
from jax.experimental.pallas import tpu as pltpu
from jax.sharding import PartitionSpec as P

REACH = 2
MESH = pl.DeviceIdType.MESH
F32 = jnp.float32
BF16 = jnp.bfloat16


def group_of(fields, rows_in, own_p):
    for group in range(1, fields + 1):
        if fields % group == 0 and group * rows_in % 16 == 0 and group * own_p % 8 == 0:
            return group
    return fields


def kernel(dims, cols_hbm, x_hbm, t_hbm, g_hbm, gm_hbm, spread_hbm, same_hbm, half_hbm, place_hbm, perm_hbm,
           out_ref, cols_ref, spread_ref, same_ref, half_ref, place_ref, perm_ref, x_all, t_all, g_all, gm_all, mix, z, contrib, part, recv, rim, halo,
           local_sem, xs, xr, fs, fr, ys, yr, hs, hr):
    n, space_size, fields, rows_in, own_p, group, modes, block_rows, slots, blk = dims
    chaos = lax.axis_index("chaos")
    mode = lax.axis_index("mode")
    space = lax.axis_index("space")
    other = 1 - mode
    above = lax.rem(space + 1, space_size)
    below = lax.rem(space + space_size - 1, space_size)
    span = block_rows + 2 * REACH
    chunks = block_rows // 2
    pairs = span // 2
    rows = fields * own_p
    p_size = n * rows_in
    shell = block_rows * space_size
    zero_at = block_rows * slots

    locals_ = [
        pltpu.make_async_copy(g_hbm.at[pl.ds(mode * modes, modes)], g_all, local_sem.at[0]),
        pltpu.make_async_copy(gm_hbm.at[pl.ds(mode * modes, modes)], gm_all, local_sem.at[1]),
        pltpu.make_async_copy(spread_hbm, spread_ref, local_sem.at[2]),
        pltpu.make_async_copy(same_hbm, same_ref, local_sem.at[3]),
        pltpu.make_async_copy(half_hbm, half_ref, local_sem.at[4]),
        pltpu.make_async_copy(place_hbm, place_ref, local_sem.at[5]),
        pltpu.make_async_copy(perm_hbm, perm_ref, local_sem.at[6]),
        pltpu.make_async_copy(cols_hbm, cols_ref, local_sem.at[7]),
        pltpu.make_async_copy(x_hbm, x_all.at[chaos], local_sem.at[8]),
    ]
    for k in range(modes):
        locals_.append(pltpu.make_async_copy(
            t_hbm.at[k], t_all.at[:, :, pl.ds(k * blk, blk)], local_sem.at[9 + k]))

    barrier = pltpu.get_barrier_semaphore()
    for d in range(1, n):
        pl.semaphore_signal(barrier, inc=1, device_id={"chaos": lax.rem(chaos + d, n)}, device_id_type=MESH)
    pl.semaphore_signal(barrier, inc=1, device_id={"mode": other}, device_id_type=MESH)
    pl.semaphore_signal(barrier, inc=1, device_id={"space": above}, device_id_type=MESH)
    pl.semaphore_signal(barrier, inc=1, device_id={"space": below}, device_id_type=MESH)
    for copy in locals_[:8]:
        copy.start()
    pl.semaphore_wait(barrier, n + 2)

    def first_row(i):
        return lax.rem(2 * i + block_rows - 2, block_rows)

    def send_x(i, d):
        cols = pl.ds(pl.multiple_of((first_row(i) + mode) * blk, blk), blk)
        return pltpu.make_async_remote_copy(
            src_ref=x_hbm.at[:, cols], dst_ref=x_all.at[chaos, :, cols],
            send_sem=xs.at[d - 1, i], recv_sem=xr.at[d - 1, i],
            device_id={"chaos": lax.rem(chaos + d, n)}, device_id_type=MESH)

    def got_x(i, d):
        source = lax.rem(chaos + n - d, n)
        cols = pl.ds(pl.multiple_of((first_row(i) + mode) * blk, blk), blk)
        return pltpu.make_async_remote_copy(
            src_ref=x_hbm.at[:, cols], dst_ref=x_all.at[source, :, cols],
            send_sem=xs.at[d - 1, i], recv_sem=xr.at[d - 1, i],
            device_id={"chaos": lax.rem(chaos + d, n)}, device_id_type=MESH)

    def forward(i, d, which):
        source = lax.rem(chaos + n - d, n)
        cols = pl.ds(pl.multiple_of((first_row(i) + which) * blk, blk), blk)
        return pltpu.make_async_remote_copy(
            src_ref=x_all.at[source, :, cols], dst_ref=x_all.at[source, :, cols],
            send_sem=fs.at[d - 1, i], recv_sem=fr.at[d - 1, i],
            device_id={"mode": other}, device_id_type=MESH)

    def first_column(q):
        return lax.rem(2 * q + span - 2, span)

    def exchange(q):
        at = pl.ds(first_column(q), 2)
        return pltpu.make_async_remote_copy(
            src_ref=part.at[at, pl.ds(rows, rows)], dst_ref=recv.at[at],
            send_sem=ys.at[q], recv_sem=yr.at[q],
            device_id={"mode": other}, device_id_type=MESH)

    def send_rim(q):
        return pltpu.make_async_remote_copy(
            src_ref=rim.at[q], dst_ref=halo.at[q],
            send_sem=hs.at[q], recv_sem=hr.at[q],
            device_id={"space": above if q == 0 else below}, device_id_type=MESH)

    def start_x(i, carry):
        for d in range(1, n):
            send_x(i, d).start()
        return carry

    lax.fori_loop(0, chunks, start_x, 0)
    for copy in locals_[8:]:
        copy.start()

    for copy in locals_[:8]:
        copy.wait()
    size_r = 2 * group * own_p
    half = half_ref[...]
    target = (2 * chaos + half * (1 - 2 * mode) + mode) * own_p + place_ref[...]
    pick = (lax.broadcasted_iota(jnp.int32, (size_r, p_size), 1) == target).astype(F32).astype(BF16)
    nt = (((1,), (1,)), ((), ()))
    for k in range(modes):
        first = lax.broadcasted_iota(jnp.int32, (p_size, p_size), 0)
        second = lax.broadcasted_iota(jnp.int32, (p_size, p_size), 1)
        value = jnp.where((first == second) | (gm_all[k] == 1), g_all[k], 0.0)
        hi = value.astype(BF16)
        lo = (value - hi.astype(F32)).astype(BF16)
        hi = lax.dot_general(pick, hi, nt, preferred_element_type=F32).astype(BF16)
        lo = lax.dot_general(pick, lo, nt, preferred_element_type=F32).astype(BF16)
        both = (jnp.dot(hi, spread_ref[0], preferred_element_type=F32)
                + jnp.dot(lo, spread_ref[1], preferred_element_type=F32))
        mix[pl.ds(k * size_r, size_r), :] = (both * same_ref[...]).astype(BF16)
    contrib[zero_at] = jnp.zeros((2 * rows, blk), F32)

    def compute(i):
        r0 = first_row(i)
        cols = pl.ds(pl.multiple_of(r0 * blk, 2 * blk), 2 * blk)
        operator = mix[...]
        pieces = []
        for g in range(fields // group):
            at = pl.ds(g * group * rows_in, group * rows_in)
            x = [x_all[s, at, cols] for s in range(n)]
            pieces.append(jnp.dot(operator, jnp.concatenate(x + x, axis=0), preferred_element_type=F32))
        part_rows = group * own_p
        for k in range(modes):
            value = jnp.concatenate([
                piece[k * size_r + h * part_rows:k * size_r + (h + 1) * part_rows]
                for h in range(2) for piece in pieces], axis=0)
            hi = value.astype(BF16)
            lo = (value - hi.astype(F32)).astype(BF16)
            for b in range(2):
                z[b, 0:2 * rows, k * blk:(k + 1) * blk] = hi[:, b * blk:(b + 1) * blk]
                z[b, 2 * rows:4 * rows, k * blk:(k + 1) * blk] = lo[:, b * blk:(b + 1) * blk]
        for b in range(2):
            right = jnp.concatenate([t_all[r0 + b, s] for s in range(slots)], axis=1)
            res = jnp.dot(z[b], right, preferred_element_type=F32)
            res = res[:2 * rows] + res[2 * rows:]
            for s in range(slots):
                contrib[(r0 + b) * slots + s] = res[:, s * blk:(s + 1) * blk]

    def combine(q):
        j0 = first_column(q)
        for e in range(2):
            column = j0 + e - REACH
            total = None
            for o in range(-REACH, REACH + 1):
                r = column - o
                inside = (r >= 0) & (r < block_rows)
                rc = jnp.clip(r, 0, block_rows - 1)
                if o == 0:
                    found = rc * slots
                else:
                    found = zero_at
                    for s in range(1, slots):
                        offset = lax.rem(cols_ref[s, rc] - (space * block_rows + rc) + shell + REACH, shell) - REACH
                        found = jnp.where(offset == o, rc * slots + s, found)
                term = contrib[jnp.where(inside, found, zero_at)]
                total = term if total is None else total + term
            part[j0 + e] = total
        exchange(q).start()

    def summed(j):
        return part[j, 0:rows] + recv[j]

    def store(column, values):
        value = jnp.concatenate([v.astype(BF16) for v in values], axis=1)
        value = jnp.dot(perm_ref[...], value, preferred_element_type=F32)
        start = column * blk
        if not isinstance(start, int):
            start = pl.multiple_of(start, 2 * blk)
        out_ref[:, pl.ds(start, 2 * blk)] = value.astype(BF16)

    def finish(q):
        exchange(q).wait()
        j0 = first_column(q)
        store(j0 - REACH, [summed(j0), summed(j0 + 1)])

    def finish_edge(q, side, column):
        exchange(q).wait()
        send_rim(side).wait()
        store(column, [summed(column + REACH + e) + halo[side, e] for e in range(2)])

    def finish_rim(q):
        exchange(q).wait()
        j0 = (2 * q + span - 2) % span
        for e in range(2):
            rim[q, e] = summed(j0 + e)
        send_rim(q).start()

    def step(t, carry):
        for d in range(1, n):
            got_x(t, d).wait_recv()
            forward(t, d, mode).start()

        @pl.when(t == 1)
        def _():
            for copy in locals_[8:]:
                copy.wait()

        @pl.when(t >= 1)
        def _():
            for d in range(1, n):
                forward(t - 1, d, other).wait_recv()
            compute(t - 1)
            combine(t - 1)

        @pl.when(t == 2)
        def _():
            finish_rim(0)

        @pl.when(t == 3)
        def _():
            finish_rim(1)

        @pl.when(t >= 5)
        def _():
            finish(t - 2)
        return carry

    lax.fori_loop(0, chunks, step, 0)
    finish_edge(2, 0, 0)
    for d in range(1, n):
        forward(chunks - 1, d, other).wait_recv()
    compute(chunks - 1)
    for q in range(chunks - 1, chunks + 2):
        combine(q)
    for q in range(chunks - 2, chunks + 1):
        finish(q)
    finish_edge(chunks + 1, 1, block_rows - 2)

    def drain(i, carry):
        for d in range(1, n):
            send_x(i, d).wait_send()
            forward(i, d, mode).wait_send()
        return carry

    lax.fori_loop(0, chunks, drain, 0)


def per_device(n, space_size, coeffs, tangent, block_cols, galerkin, galerkin_mask):
    fields, rows_in, tile = coeffs.shape
    modes, block_rows, slots, blk, _ = tangent.shape
    p_size = galerkin.shape[1]
    own_p = p_size // (2 * n)
    group = group_of(fields, rows_in, own_p)
    rows = fields * own_p
    width = n * group * rows_in
    span = block_rows + 2 * REACH
    chunks = block_rows // 2
    size_r = 2 * group * own_p

    src, fld, q = np.meshgrid(np.arange(n), np.arange(group), np.arange(rows_in), indexing="ij")
    q_of = (src * rows_in + q).reshape(-1)
    one = (np.arange(p_size)[:, None] == q_of[None, :]).astype(np.float32)
    nil = np.zeros_like(one)
    spread = jnp.asarray(np.stack([np.concatenate([one, nil], 1), np.concatenate([nil, one], 1)]), BF16)
    h_of, f_of, p_of = (a.reshape(-1) for a in np.meshgrid(np.arange(2), np.arange(group), np.arange(own_p), indexing="ij"))
    same = jnp.asarray((f_of[:, None] == np.tile(fld.reshape(-1), 2)[None, :]).astype(np.float32))
    half = jnp.asarray(np.repeat(h_of[:, None], p_size, 1).astype(np.int32))
    place = jnp.asarray(np.repeat(p_of[:, None], p_size, 1).astype(np.int32))
    to = np.arange(rows)
    source = (to % fields) * own_p + to // fields
    perm = jnp.asarray((source[:, None] == np.arange(rows)[None, :]).astype(np.float32), BF16)

    dims = (n, space_size, fields, rows_in, own_p, group, modes, block_rows, slots, blk)
    hbm = pl.BlockSpec(memory_space=pltpu.HBM)
    out = pl.pallas_call(
        functools.partial(kernel, dims),
        out_shape=pltpu.VMEM((rows, tile), BF16),
        in_specs=[hbm] * 10,
        scratch_shapes=[
            pltpu.SMEM((slots, block_rows), jnp.int32),
            pltpu.VMEM(spread.shape, BF16),
            pltpu.VMEM(same.shape, F32),
            pltpu.VMEM(half.shape, jnp.int32),
            pltpu.VMEM(place.shape, jnp.int32),
            pltpu.VMEM(perm.shape, BF16),
            pltpu.VMEM((n, fields * rows_in, tile), BF16),
            pltpu.VMEM((block_rows, slots, modes * blk, blk), BF16),
            pltpu.VMEM((modes, p_size, p_size), F32),
            pltpu.VMEM((modes, p_size, p_size), jnp.int32),
            pltpu.VMEM((modes * size_r, 2 * width), BF16),
            pltpu.VMEM((2, 4 * rows, modes * blk), BF16),
            pltpu.VMEM((block_rows * slots + 1, 2 * rows, blk), F32),
            pltpu.VMEM((span, 2 * rows, blk), F32),
            pltpu.VMEM((span, rows, blk), F32),
            pltpu.VMEM((2, REACH, rows, blk), F32),
            pltpu.VMEM((2, REACH, rows, blk), F32),
            pltpu.SemaphoreType.DMA((9 + modes,)),
            pltpu.SemaphoreType.DMA((n - 1, chunks)),
            pltpu.SemaphoreType.DMA((n - 1, chunks)),
            pltpu.SemaphoreType.DMA((n - 1, chunks)),
            pltpu.SemaphoreType.DMA((n - 1, chunks)),
            pltpu.SemaphoreType.DMA((chunks + 2,)),
            pltpu.SemaphoreType.DMA((chunks + 2,)),
            pltpu.SemaphoreType.DMA((2,)),
            pltpu.SemaphoreType.DMA((2,)),
        ],
        compiler_params=pltpu.CompilerParams(
            collective_id=0, has_side_effects=True, vmem_limit_bytes=60 * 1024 * 1024),
    )(block_cols.T, coeffs.reshape(fields * rows_in, tile), tangent, galerkin, galerkin_mask,
      spread, same, half, place, perm)
    return jnp.transpose(out.reshape(own_p, fields, tile), (1, 0, 2))


def solution(mesh):
    return jax.shard_map(
        functools.partial(per_device, mesh.shape["chaos"], mesh.shape["space"]),
        mesh=mesh,
        in_specs=(
            P(None, "chaos", ("grp", "space")),
            P("mode", ("grp", "space"), None, None, None),
            P(("grp", "space"), None),
            P(),
            P(),
        ),
        out_specs=P(None, ("chaos", "mode"), ("grp", "space")),
        check_vma=False,
    )
```

```python
import functools

import jax
import jax.numpy as jnp
import numpy as np
from jax import lax
from jax.experimental import pallas as pl
from jax.experimental.pallas import tpu as pltpu
from jax.sharding import PartitionSpec as P

REACH = 2
MESH = pl.DeviceIdType.MESH
F32 = jnp.float32
BF16 = jnp.bfloat16


def group_of(fields, rows_in, own_p):
    for group in range(1, fields + 1):
        if fields % group == 0 and group * rows_in % 16 == 0 and group * own_p % 8 == 0:
            return group
    return fields


def kernel(dims, cols_hbm, x_hbm, t_hbm, g_hbm, gm_hbm, spread_hbm, same_hbm, half_hbm, place_hbm, perm_hbm,
           out_ref, cols_ref, spread_ref, same_ref, half_ref, place_ref, perm_ref, x_all, t_all, g_all, gm_all, mix, z, contrib, part, recv, rim, halo,
           local_sem, xs, xr, fs, fr, ys, yr, hs, hr):
    n, space_size, fields, rows_in, own_p, group, modes, block_rows, slots, blk = dims
    chaos = lax.axis_index("chaos")
    mode = lax.axis_index("mode")
    space = lax.axis_index("space")
    other = 1 - mode
    above = lax.rem(space + 1, space_size)
    below = lax.rem(space + space_size - 1, space_size)
    span = block_rows + 2 * REACH
    chunks = block_rows // 2
    pairs = span // 2
    rows = fields * own_p
    p_size = n * rows_in
    shell = block_rows * space_size
    zero_at = block_rows * slots

    locals_ = [
        pltpu.make_async_copy(g_hbm.at[pl.ds(mode * modes, modes)], g_all, local_sem.at[0]),
        pltpu.make_async_copy(gm_hbm.at[pl.ds(mode * modes, modes)], gm_all, local_sem.at[1]),
        pltpu.make_async_copy(spread_hbm, spread_ref, local_sem.at[2]),
        pltpu.make_async_copy(same_hbm, same_ref, local_sem.at[3]),
        pltpu.make_async_copy(half_hbm, half_ref, local_sem.at[4]),
        pltpu.make_async_copy(place_hbm, place_ref, local_sem.at[5]),
        pltpu.make_async_copy(perm_hbm, perm_ref, local_sem.at[6]),
        pltpu.make_async_copy(cols_hbm, cols_ref, local_sem.at[7]),
        pltpu.make_async_copy(x_hbm, x_all.at[chaos], local_sem.at[8]),
    ]
    for k in range(modes):
        locals_.append(pltpu.make_async_copy(
            t_hbm.at[k], t_all.at[:, :, pl.ds(k * blk, blk)], local_sem.at[9 + k]))

    barrier = pltpu.get_barrier_semaphore()
    for d in range(1, n):
        pl.semaphore_signal(barrier, inc=1, device_id={"chaos": lax.rem(chaos + d, n)}, device_id_type=MESH)
    pl.semaphore_signal(barrier, inc=1, device_id={"mode": other}, device_id_type=MESH)
    pl.semaphore_signal(barrier, inc=1, device_id={"space": above}, device_id_type=MESH)
    pl.semaphore_signal(barrier, inc=1, device_id={"space": below}, device_id_type=MESH)
    for copy in locals_[:9]:
        copy.start()
    pl.semaphore_wait(barrier, n + 2)

    def first_row(i):
        return lax.rem(2 * i + block_rows - 2, block_rows)

    def send_x(i, d):
        cols = pl.ds(pl.multiple_of((first_row(i) + mode) * blk, blk), blk)
        return pltpu.make_async_remote_copy(
            src_ref=x_all.at[chaos, :, cols], dst_ref=x_all.at[chaos, :, cols],
            send_sem=xs.at[d - 1, i], recv_sem=xr.at[d - 1, i],
            device_id={"chaos": lax.rem(chaos + d, n)}, device_id_type=MESH)

    def got_x(i, d):
        source = lax.rem(chaos + n - d, n)
        cols = pl.ds(pl.multiple_of((first_row(i) + mode) * blk, blk), blk)
        return pltpu.make_async_remote_copy(
            src_ref=x_all.at[chaos, :, cols], dst_ref=x_all.at[source, :, cols],
            send_sem=xs.at[d - 1, i], recv_sem=xr.at[d - 1, i],
            device_id={"chaos": lax.rem(chaos + d, n)}, device_id_type=MESH)

    def forward(i, d, which):
        source = lax.rem(chaos + n - d, n)
        cols = pl.ds(pl.multiple_of((first_row(i) + which) * blk, blk), blk)
        return pltpu.make_async_remote_copy(
            src_ref=x_all.at[source, :, cols], dst_ref=x_all.at[source, :, cols],
            send_sem=fs.at[d - 1, i], recv_sem=fr.at[d - 1, i],
            device_id={"mode": other}, device_id_type=MESH)

    def first_column(q):
        return lax.rem(2 * q + span - 2, span)

    def exchange(q):
        at = pl.ds(first_column(q), 2)
        return pltpu.make_async_remote_copy(
            src_ref=part.at[at, pl.ds(rows, rows)], dst_ref=recv.at[at],
            send_sem=ys.at[q], recv_sem=yr.at[q],
            device_id={"mode": other}, device_id_type=MESH)

    def send_rim(q):
        return pltpu.make_async_remote_copy(
            src_ref=rim.at[q], dst_ref=halo.at[q],
            send_sem=hs.at[q], recv_sem=hr.at[q],
            device_id={"space": above if q == 0 else below}, device_id_type=MESH)

    def start_x(i, carry):
        for d in range(1, n):
            send_x(i, d).start()
        return carry

    locals_[8].wait()
    lax.fori_loop(0, chunks, start_x, 0)
    for copy in locals_[9:]:
        copy.start()

    for copy in locals_[:8]:
        copy.wait()
    size_r = 2 * group * own_p
    half = half_ref[...]
    target = (2 * chaos + half * (1 - 2 * mode) + mode) * own_p + place_ref[...]
    pick = (lax.broadcasted_iota(jnp.int32, (size_r, p_size), 1) == target).astype(F32).astype(BF16)
    nt = (((1,), (1,)), ((), ()))
    for k in range(modes):
        first = lax.broadcasted_iota(jnp.int32, (p_size, p_size), 0)
        second = lax.broadcasted_iota(jnp.int32, (p_size, p_size), 1)
        value = jnp.where((first == second) | (gm_all[k] == 1), g_all[k], 0.0)
        hi = value.astype(BF16)
        lo = (value - hi.astype(F32)).astype(BF16)
        hi = lax.dot_general(pick, hi, nt, preferred_element_type=F32).astype(BF16)
        lo = lax.dot_general(pick, lo, nt, preferred_element_type=F32).astype(BF16)
        both = (jnp.dot(hi, spread_ref[0], preferred_element_type=F32)
                + jnp.dot(lo, spread_ref[1], preferred_element_type=F32))
        mix[pl.ds(k * size_r, size_r), :] = (both * same_ref[...]).astype(BF16)
    contrib[zero_at] = jnp.zeros((2 * rows, blk), F32)

    def compute(i):
        r0 = first_row(i)
        cols = pl.ds(pl.multiple_of(r0 * blk, 2 * blk), 2 * blk)
        operator = mix[...]
        pieces = []
        for g in range(fields // group):
            at = pl.ds(g * group * rows_in, group * rows_in)
            x = [x_all[s, at, cols] for s in range(n)]
            pieces.append(jnp.dot(operator, jnp.concatenate(x + x, axis=0), preferred_element_type=F32))
        part_rows = group * own_p
        for k in range(modes):
            value = jnp.concatenate([
                piece[k * size_r + h * part_rows:k * size_r + (h + 1) * part_rows]
                for h in range(2) for piece in pieces], axis=0)
            hi = value.astype(BF16)
            lo = (value - hi.astype(F32)).astype(BF16)
            for b in range(2):
                z[b, 0:2 * rows, k * blk:(k + 1) * blk] = hi[:, b * blk:(b + 1) * blk]
                z[b, 2 * rows:4 * rows, k * blk:(k + 1) * blk] = lo[:, b * blk:(b + 1) * blk]
        for b in range(2):
            right = jnp.concatenate([t_all[r0 + b, s] for s in range(slots)], axis=1)
            res = jnp.dot(z[b], right, preferred_element_type=F32)
            res = res[:2 * rows] + res[2 * rows:]
            for s in range(slots):
                contrib[(r0 + b) * slots + s] = res[:, s * blk:(s + 1) * blk]

    def combine(q):
        j0 = first_column(q)
        for e in range(2):
            column = j0 + e - REACH
            total = None
            for o in range(-REACH, REACH + 1):
                r = column - o
                inside = (r >= 0) & (r < block_rows)
                rc = jnp.clip(r, 0, block_rows - 1)
                if o == 0:
                    found = rc * slots
                else:
                    found = zero_at
                    for s in range(1, slots):
                        offset = lax.rem(cols_ref[s, rc] - (space * block_rows + rc) + shell + REACH, shell) - REACH
                        found = jnp.where(offset == o, rc * slots + s, found)
                term = contrib[jnp.where(inside, found, zero_at)]
                total = term if total is None else total + term
            part[j0 + e] = total
        exchange(q).start()

    def summed(j):
        return part[j, 0:rows] + recv[j]

    def store(column, values):
        value = jnp.concatenate([v.astype(BF16) for v in values], axis=1)
        value = jnp.dot(perm_ref[...], value, preferred_element_type=F32)
        start = column * blk
        if not isinstance(start, int):
            start = pl.multiple_of(start, 2 * blk)
        out_ref[:, pl.ds(start, 2 * blk)] = value.astype(BF16)

    def finish(q):
        exchange(q).wait()
        j0 = first_column(q)
        store(j0 - REACH, [summed(j0), summed(j0 + 1)])

    def finish_edge(q, side, column):
        exchange(q).wait()
        send_rim(side).wait()
        store(column, [summed(column + REACH + e) + halo[side, e] for e in range(2)])

    def finish_rim(q):
        exchange(q).wait()
        j0 = (2 * q + span - 2) % span
        for e in range(2):
            rim[q, e] = summed(j0 + e)
        send_rim(q).start()

    def step(t, carry):
        for d in range(1, n):
            got_x(t, d).wait_recv()
            forward(t, d, mode).start()

        @pl.when(t == 1)
        def _():
            for copy in locals_[9:]:
                copy.wait()

        @pl.when(t >= 1)
        def _():
            for d in range(1, n):
                forward(t - 1, d, other).wait_recv()
            compute(t - 1)
            combine(t - 1)

        @pl.when(t == 2)
        def _():
            finish_rim(0)

        @pl.when(t == 3)
        def _():
            finish_rim(1)

        @pl.when(t >= 5)
        def _():
            finish(t - 2)
        return carry

    lax.fori_loop(0, chunks, step, 0)
    finish_edge(2, 0, 0)
    for d in range(1, n):
        forward(chunks - 1, d, other).wait_recv()
    compute(chunks - 1)
    for q in range(chunks - 1, chunks + 2):
        combine(q)
    for q in range(chunks - 2, chunks + 1):
        finish(q)
    finish_edge(chunks + 1, 1, block_rows - 2)

    def drain(i, carry):
        for d in range(1, n):
            send_x(i, d).wait_send()
            forward(i, d, mode).wait_send()
        return carry

    lax.fori_loop(0, chunks, drain, 0)


def per_device(n, space_size, coeffs, tangent, block_cols, galerkin, galerkin_mask):
    fields, rows_in, tile = coeffs.shape
    modes, block_rows, slots, blk, _ = tangent.shape
    p_size = galerkin.shape[1]
    own_p = p_size // (2 * n)
    group = group_of(fields, rows_in, own_p)
    rows = fields * own_p
    width = n * group * rows_in
    span = block_rows + 2 * REACH
    chunks = block_rows // 2
    size_r = 2 * group * own_p

    src, fld, q = np.meshgrid(np.arange(n), np.arange(group), np.arange(rows_in), indexing="ij")
    q_of = (src * rows_in + q).reshape(-1)
    one = (np.arange(p_size)[:, None] == q_of[None, :]).astype(np.float32)
    nil = np.zeros_like(one)
    spread = jnp.asarray(np.stack([np.concatenate([one, nil], 1), np.concatenate([nil, one], 1)]), BF16)
    h_of, f_of, p_of = (a.reshape(-1) for a in np.meshgrid(np.arange(2), np.arange(group), np.arange(own_p), indexing="ij"))
    same = jnp.asarray((f_of[:, None] == np.tile(fld.reshape(-1), 2)[None, :]).astype(np.float32))
    half = jnp.asarray(np.repeat(h_of[:, None], p_size, 1).astype(np.int32))
    place = jnp.asarray(np.repeat(p_of[:, None], p_size, 1).astype(np.int32))
    to = np.arange(rows)
    source = (to % fields) * own_p + to // fields
    perm = jnp.asarray((source[:, None] == np.arange(rows)[None, :]).astype(np.float32), BF16)

    dims = (n, space_size, fields, rows_in, own_p, group, modes, block_rows, slots, blk)
    hbm = pl.BlockSpec(memory_space=pltpu.HBM)
    out = pl.pallas_call(
        functools.partial(kernel, dims),
        out_shape=pltpu.VMEM((rows, tile), BF16),
        in_specs=[hbm] * 10,
        scratch_shapes=[
            pltpu.SMEM((slots, block_rows), jnp.int32),
            pltpu.VMEM(spread.shape, BF16),
            pltpu.VMEM(same.shape, F32),
            pltpu.VMEM(half.shape, jnp.int32),
            pltpu.VMEM(place.shape, jnp.int32),
            pltpu.VMEM(perm.shape, BF16),
            pltpu.VMEM((n, fields * rows_in, tile), BF16),
            pltpu.VMEM((block_rows, slots, modes * blk, blk), BF16),
            pltpu.VMEM((modes, p_size, p_size), F32),
            pltpu.VMEM((modes, p_size, p_size), jnp.int32),
            pltpu.VMEM((modes * size_r, 2 * width), BF16),
            pltpu.VMEM((2, 4 * rows, modes * blk), BF16),
            pltpu.VMEM((block_rows * slots + 1, 2 * rows, blk), F32),
            pltpu.VMEM((span, 2 * rows, blk), F32),
            pltpu.VMEM((span, rows, blk), F32),
            pltpu.VMEM((2, REACH, rows, blk), F32),
            pltpu.VMEM((2, REACH, rows, blk), F32),
            pltpu.SemaphoreType.DMA((9 + modes,)),
            pltpu.SemaphoreType.DMA((n - 1, chunks)),
            pltpu.SemaphoreType.DMA((n - 1, chunks)),
            pltpu.SemaphoreType.DMA((n - 1, chunks)),
            pltpu.SemaphoreType.DMA((n - 1, chunks)),
            pltpu.SemaphoreType.DMA((chunks + 2,)),
            pltpu.SemaphoreType.DMA((chunks + 2,)),
            pltpu.SemaphoreType.DMA((2,)),
            pltpu.SemaphoreType.DMA((2,)),
        ],
        compiler_params=pltpu.CompilerParams(
            collective_id=0, has_side_effects=True, vmem_limit_bytes=60 * 1024 * 1024),
    )(block_cols.T, coeffs.reshape(fields * rows_in, tile), tangent, galerkin, galerkin_mask,
      spread, same, half, place, perm)
    return jnp.transpose(out.reshape(own_p, fields, tile), (1, 0, 2))


def solution(mesh):
    return jax.shard_map(
        functools.partial(per_device, mesh.shape["chaos"], mesh.shape["space"]),
        mesh=mesh,
        in_specs=(
            P(None, "chaos", ("grp", "space")),
            P("mode", ("grp", "space"), None, None, None),
            P(("grp", "space"), None),
            P(),
            P(),
        ),
        out_specs=P(None, ("chaos", "mode"), ("grp", "space")),
        check_vma=False,
    )
```
